32 devices in a mesh: groups: 2 (over y), seq: 4 (over x, core), tm: 4 (over z).
Axes of the slice: x: 2, y: 2, z: 4, core: 2. Of those that a mesh axis runs over, the one named last changes fastest.
Arguments:
- init_latent: float32 [32, 512], P('groups', 'seq'), parts along dimension 0, may hold values from -6 to 6
- cur_ids: int32 [4], P('tm'), may hold values from 1 to 999, as said below
- next_ids: int32 [4], P('tm'), may hold values from 0 to 998, as said below
- beta_table: float32 [1000], replicated, may hold values from 0.0002 to 0.008
- temb_weight: bfloat16 [256, 1152], replicated, may hold values from -0.375 to 0.375
- mod_weight: bfloat16 [1152, 5, 1152], P('seq'), may hold values from -0.1875 to 0.1875
- mod_bias: float32 [5, 1152], replicated, may hold values from -3 to 3
- patch_weight: float32 [16, 1152], replicated, may hold values from -1.5 to 1.5
- qkv_weight: bfloat16 [1152, 3, 1152], P('tm', None, 'seq'), may hold values from -6 to 6
- out_weight: bfloat16 [1152, 1152], P(None, 'tm'), may hold values from -0.1875 to 0.1875
- final_weight: bfloat16 [1152, 16], replicated, may hold values from -0.1875 to 0.1875
Outputs:
- trajectory: float32 [4, 32, 512], P('tm', 'groups', 'seq'), parts along dimension 1
- noise_pred: float32 [4, 32, 512], P('tm', 'groups', 'seq'), parts along dimension 1
The draws below stay inside these ranges and needn't reach their ends.
There are 2 independent parts, one for each index of `groups`. The reference program is written for one: setup_inputs(seed, part) draws one part's arguments, and reference() takes and returns one part's arrays. A program takes and returns all parts, laid end to end along the dimension named above; an argument that names none is the same for every part. Nothing has to cross between parts.
Inputs may be any that keep to these rules, and one draw needn't show every extreme that they name: `cur_ids`: strictly falling along the steps; the first is 999. next_ids[t] = cur_ids[t + 1] for t < 3, and the last is 0.
All inputs are finite; a program needn't handle non-finite values.
Results may differ from the reference program's by a relative error of at most 0.006.
Values may be sent and summed in bfloat16 or wider, within the bound.
A program may use at most 128 MiB of HBM per device.

```python
import math
import jax
import jax.numpy as jnp
from jax import lax

D = 1152
HEADS = 16
CH = 16
FREQ = 256
MODS = 5
TABLE = 1000
ITERS = 3
STEPS = 4
SEQ = 512


def plan_ids(key):
    middle = jax.random.permutation(jax.random.fold_in(key, 11), TABLE - 4)[:STEPS - 3] + 2
    inner = jnp.concatenate([middle, jnp.array([1, TABLE - 2], dtype=middle.dtype)])
    falling = -jnp.sort(-inner)
    whole = jnp.concatenate([jnp.full((1,), TABLE - 1, dtype=falling.dtype), falling, jnp.zeros((1,), dtype=falling.dtype)])
    return whole.astype(jnp.int32)


def draw_cur_ids(key, part):
    return plan_ids(key)[:STEPS]


def draw_next_ids(key, part):
    return plan_ids(key)[1:]


def draw_init_latent(key, part):
    values = jax.random.normal(jax.random.fold_in(key, 5), (CH, SEQ), dtype=jnp.float32)
    return jnp.clip(values, -6.0, 6.0)


def draw_qkv_weight(key, part):
    base = jax.random.normal(jax.random.fold_in(key, 21), (D, 3, D), dtype=jnp.float32) / math.sqrt(D)
    return jnp.clip(base, -6.0, 6.0).astype(jnp.bfloat16)


def block_levels(rng, dims, cuts, low, top_value):
    loudness = 1.0
    for dim, parts in cuts:
        heights = jax.random.uniform(jax.random.fold_in(jax.random.fold_in(rng, 6), dim), (parts,), jnp.float32, low / len(cuts), top_value / len(cuts))
        loudness = loudness * jnp.repeat(jnp.exp(heights), dims[dim] // parts).reshape((-1,) + (1,) * (len(dims) - 1 - dim))
    return loudness


def gaussian(key, shape, scale, reach, pieces=(), held_as=jnp.bfloat16):
    loudness = block_levels(key, shape, pieces, -0.22, 0.18) if pieces else 1.0
    result = jax.random.normal(key, shape, jnp.float32) * scale * loudness
    return jnp.minimum(jnp.maximum(result, -reach), reach).astype(held_as)


def setup_inputs(seed: int = 0, part: int = 0) -> dict:
    keys = jax.random.split(jax.random.key(seed), 12)
    own_keys = jax.random.split(jax.random.fold_in(keys[11], part), 12)
    return {
        "init_latent": draw_init_latent(jax.random.fold_in(jax.random.fold_in(keys[11], part), 71), part),
        "cur_ids": draw_cur_ids(jax.random.fold_in(keys[11], 71), part),
        "next_ids": draw_next_ids(jax.random.fold_in(keys[11], 71), part),
        "beta_table": jnp.clip(jnp.exp(jax.random.uniform(keys[3], (TABLE,), jnp.float32, math.log(0.0002), math.log(0.008))), 0.0002, 0.008),
        "temb_weight": gaussian(keys[4], (FREQ, D), FREQ ** -0.5, 0.375),
        "mod_weight": gaussian(keys[5], (D, MODS, D), D ** -0.5, 0.1875, ((0, 4),)),
        "mod_bias": gaussian(keys[6], (MODS, D), 0.5, 3.0, (), jnp.float32),
        "patch_weight": gaussian(keys[7], (CH, D), CH ** -0.5, 1.5, (), jnp.float32),
        "qkv_weight": draw_qkv_weight(jax.random.fold_in(keys[11], 71), part),
        "out_weight": gaussian(keys[9], (D, D), D ** -0.5, 0.1875, ((1, 4),)),
        "final_weight": gaussian(keys[10], (D, CH), D ** -0.5, 0.1875),
    }


def layer_norm(values):
    center = values - lax.optimization_barrier(jnp.mean(values, axis=-1, keepdims=True))
    spread = lax.optimization_barrier(jnp.mean(center * center, axis=-1, keepdims=True))
    return center / jnp.sqrt(spread + 1e-06)

def plan_coefs(beta_table, cur_ids, next_ids):
    alpha_bar = jnp.cumprod(1.0 - beta_table)
    table_pos = jnp.arange(beta_table.shape[0], dtype=jnp.int32)
    bar_now = lax.optimization_barrier(jnp.sum(jnp.where(table_pos[None, :] == cur_ids[:, None], alpha_bar[None, :], 0.0), axis=1))
    bar_next = lax.optimization_barrier(jnp.sum(jnp.where(table_pos[None, :] == next_ids[:, None], alpha_bar[None, :], 0.0), axis=1))
    coef_a = jnp.sqrt(bar_next / bar_now)
    coef_b = jnp.sqrt(1.0 - bar_next) - coef_a * jnp.sqrt(1.0 - bar_now)
    return (coef_a, coef_b)

def frequency_embed(cur_ids, freq_width):
    half_width = freq_width // 2
    frequencies = jnp.exp(-math.log(10000.0) * jnp.arange(half_width, dtype=jnp.float32) / half_width)
    angles = cur_ids.astype(jnp.float32)[:, None] * frequencies[None, :]
    return jnp.concatenate([jnp.cos(angles), jnp.sin(angles)], axis=1)

def predict(latent_state, modulation, patch_weight, qkv_weight, out_weight, final_weight):
    embedded = lax.dot_general(latent_state, patch_weight, (((0,), (0,)), ((), ())), precision=lax.Precision.HIGHEST)
    normed = (layer_norm(embedded) * (1.0 + modulation[1]) + modulation[0]).astype(jnp.bfloat16)
    seq_len = embedded.shape[0]
    head_dim = D // HEADS
    proj_qkv = jnp.dot(normed, qkv_weight.reshape(D, 3 * D), preferred_element_type=jnp.float32).astype(jnp.bfloat16)
    proj_qkv = proj_qkv.reshape(seq_len, 3, HEADS, head_dim).astype(jnp.float32)
    scores = jnp.einsum('qhe,khe->hqk', proj_qkv[:, 0], proj_qkv[:, 1]) / math.sqrt(head_dim)
    scores = scores - lax.optimization_barrier(jnp.max(scores, axis=-1, keepdims=True))
    weights = jnp.exp(scores)
    attn_probs = (weights / lax.optimization_barrier(jnp.sum(weights, axis=-1, keepdims=True))).astype(jnp.bfloat16)
    heads_out = jnp.einsum('hqk,khe->qhe', attn_probs.astype(jnp.float32), proj_qkv[:, 2])
    heads_out = heads_out.astype(jnp.bfloat16).reshape(seq_len, D)
    projected = jnp.dot(heads_out, out_weight, preferred_element_type=jnp.float32)
    residual = embedded + modulation[2] * projected
    final_in = (layer_norm(residual) * (1.0 + modulation[4]) + modulation[3]).astype(jnp.bfloat16)
    return lax.dot_general(final_weight, final_in, (((0,), (1,)), ((), ())), preferred_element_type=jnp.float32)

def reference(init_latent, cur_ids, next_ids, beta_table, temb_weight, mod_weight, mod_bias, patch_weight, qkv_weight, out_weight, final_weight):
    coef_a, coef_b = plan_coefs(beta_table, cur_ids, next_ids)
    freq_emb = frequency_embed(cur_ids, FREQ).astype(jnp.bfloat16)
    time_emb = jax.nn.silu(jnp.dot(freq_emb, temb_weight, preferred_element_type=jnp.float32)).astype(jnp.bfloat16)
    mod_raw = jnp.dot(time_emb, mod_weight.reshape(D, MODS * D), preferred_element_type=jnp.float32).astype(jnp.bfloat16)
    modulation = mod_raw.reshape(STEPS, MODS, D).astype(jnp.float32) + mod_bias[None]
    states = jnp.broadcast_to(init_latent[None], (STEPS, CH, init_latent.shape[1]))
    noise_pred = jnp.zeros_like(states)
    for iteration in range(ITERS):
        noise_pred = lax.map(lambda inputs_pair: predict(inputs_pair[0], inputs_pair[1], patch_weight, qkv_weight, out_weight, final_weight), (states, modulation))
        drift_term = (coef_a - 1.0)[:, None, None] * states + coef_b[:, None, None] * noise_pred
        states = init_latent[None] + (jnp.cumsum(drift_term, axis=0) - drift_term)
    return (states, noise_pred)
```

```python
import functools
import math

import jax
import jax.numpy as jnp
from jax import lax
from jax.experimental import pallas as pl
from jax.experimental.pallas import tpu as pltpu
from jax.sharding import PartitionSpec as P

HEADS = 16
ITERS = 3
AUG = 24
HIGH = lax.Precision.HIGHEST
MESH = pl.DeviceIdType.MESH
F32, BF16 = jnp.float32, jnp.bfloat16


def greet(plan):
    barrier = pltpu.get_barrier_semaphore()
    total = 0
    for axis, n in plan:
        me = lax.axis_index(axis)
        for d in range(1, n):
            pl.semaphore_signal(
                barrier, inc=1, device_id={axis: lax.rem(me + d, n)}, device_id_type=MESH
            )
        total += n - 1
    pl.semaphore_wait(barrier, total)


def sends(axis, n, source, landing, send, recv, scatter=False):
    me = lax.axis_index(axis)
    copies = []
    for d in range(1, n):
        peer = lax.rem(me + d, n)
        copies.append(
            pltpu.make_async_remote_copy(
                src_ref=source.at[peer] if scatter else source,
                dst_ref=landing.at[me],
                send_sem=send.at[d - 1],
                recv_sem=recv.at[d - 1],
                device_id={axis: peer},
                device_id_type=MESH,
            )
        )
    return copies


def exchange_kernel(axis, n, scatter, count, *refs):
    sources, landings = refs[:count], refs[count : 2 * count]
    send, recv = refs[2 * count :]
    greet([(axis, n)])
    me = lax.axis_index(axis)
    copies = []
    for i in range(count):
        copies += sends(axis, n, sources[i], landings[i], send.at[i], recv.at[i], scatter)
    for copy in copies:
        copy.start()
    for source, landing in zip(sources, landings):
        landing[me] = source[me] if scatter else source[...]
    for copy in copies:
        copy.wait()


def exchange(values, axis, cid, scatter=False):
    n = lax.axis_size(axis)
    count = len(values)
    shapes = [v.shape if scatter else (n,) + v.shape for v in values]
    vmem = pl.BlockSpec(memory_space=pltpu.VMEM)
    return pl.pallas_call(
        functools.partial(exchange_kernel, axis, n, scatter, count),
        out_shape=[jax.ShapeDtypeStruct(s, v.dtype) for s, v in zip(shapes, values)],
        in_specs=[vmem] * count,
        out_specs=[vmem] * count,
        scratch_shapes=[
            pltpu.SemaphoreType.DMA((count, n - 1)),
            pltpu.SemaphoreType.DMA((count, n - 1)),
        ],
        compiler_params=pltpu.CompilerParams(
            collective_id=cid, has_side_effects=True, vmem_limit_bytes=40 << 20
        ),
    )(*values)


def split(value):
    high = value.astype(BF16).astype(F32)
    return high, value - high


def picard_kernel(
    n_seq, n_tm,
    z0_ref, coef_ref, patch_ref, fmod_ref, final_ref, a_ref, big_ref,
    traj_ref, noise_ref,
    state, ubuf, dbuf, usrc, dsrc, yrows, usend, urecv, dsend, drecv,
):
    greet([("seq", n_seq), ("tm", n_tm)])
    here, when = lax.axis_index("seq"), lax.axis_index("tm")
    ch, tok = z0_ref.shape
    width = big_ref.shape[1]
    keys = n_seq * tok
    block = big_ref.shape[0] // n_seq
    heads_here = HEADS // n_seq
    state[...] = z0_ref[...]

    def ones_tail(lanes):
        row = lax.broadcasted_iota(jnp.int32, (AUG - ch, lanes), 0)
        return jnp.where(row == 0, 1.0, 0.0).astype(F32)

    row = lax.broadcasted_iota(jnp.int32, (16, 2 * tok), 0)
    lane = lax.broadcasted_iota(jnp.int32, (16, 2 * tok), 1)
    const = jnp.where((row == 0) & (lane < tok), 1.0, 0.0).astype(BF16)
    for s in range(n_seq):
        yrows[s * block + heads_here * 16 : (s + 1) * block, :] = const

    def one(it, carry):
        z = state[...]
        emb = lax.dot_general(
            patch_ref[...], z, (((1,), (0,)), ((), ())),
            precision=HIGH, preferred_element_type=F32,
        )
        center = emb - jnp.mean(emb, axis=0, keepdims=True)
        spread = jnp.mean(center * center, axis=0, keepdims=True)
        u = z / jnp.sqrt(spread + 1e-06)
        usrc[it] = u
        copies = sends("seq", n_seq, usrc.at[it], ubuf.at[it], usend.at[it], urecv.at[it])
        for copy in copies:
            copy.start()
        ubuf[it, here] = u
        u_query = jnp.concatenate([u, ones_tail(tok)], axis=0)
        g = lax.dot_general(
            a_ref[...], u_query, (((1,), (0,)), ((), ())),
            precision=HIGH, preferred_element_type=F32,
        )
        for copy in copies:
            copy.wait()
        u_all = jnp.concatenate([ubuf[it, s] for s in range(n_seq)], axis=1)
        u_keys = jnp.concatenate([u_all, ones_tail(keys)], axis=0)
        k_high, k_low = split(u_keys)
        pad = jnp.zeros((128 - 3 * AUG, keys), F32)
        key_rows = jnp.transpose(jnp.concatenate([k_high, k_high, k_low, pad], axis=0)).astype(BF16)
        values = jnp.concatenate([k_high, k_low], axis=0).astype(BF16)
        qpad = jnp.zeros((128 - 3 * AUG, 2 * tok), F32)
        for pair in range(HEADS // 2):
            lo = pair * 2 * AUG
            both = jnp.concatenate([g[lo : lo + AUG], g[lo + AUG : lo + 2 * AUG]], axis=1)
            q_high, q_low = split(both)
            query = jnp.concatenate([q_high, q_low, q_high, qpad], axis=0).astype(BF16)
            scores = jnp.dot(key_rows, query, preferred_element_type=F32)
            top = jnp.max(scores, axis=0, keepdims=True)
            probs = jnp.exp2(scores - top).astype(BF16)
            out = jnp.dot(values, probs, preferred_element_type=F32)
            out = out[:AUG] + out[AUG:]
            y_high, y_low = split(out[:ch] / out[ch : ch + 1])
            for k in range(2):
                head = pair * 2 + k
                at = head // heads_here * block + head % heads_here * 16
                cut = slice(k * tok, (k + 1) * tok)
                yrows[at : at + 16, 0:tok] = y_high[:, cut].astype(BF16)
                yrows[at : at + 16, tok : 2 * tok] = y_low[:, cut].astype(BF16)
        proj = lax.dot_general(
            big_ref[...], yrows[...], (((0,), (0,)), ((), ())), preferred_element_type=F32
        )
        residual = emb + proj[:, :tok] + proj[:, tok:]
        center = residual - jnp.mean(residual, axis=0, keepdims=True)
        spread = jnp.mean(center * center, axis=0, keepdims=True)
        normed = center / jnp.sqrt(spread + 1e-06)
        final_in = (normed * fmod_ref[:, 0:1] + fmod_ref[:, 1:2]).astype(BF16)
        noise = jnp.dot(final_ref[...], final_in, preferred_element_type=F32)
        noise_ref[...] = noise
        drift = coef_ref[0] * z + coef_ref[1] * noise
        dsrc[it] = drift
        copies = sends("tm", n_tm, dsrc.at[it], dbuf.at[it], dsend.at[it], drecv.at[it])
        for copy in copies:
            copy.start()
        dbuf[it, when] = drift
        for copy in copies:
            copy.wait()
        total = jnp.zeros_like(drift)
        for j in range(n_tm - 1):
            total = total + jnp.where(when > j, dbuf[it, j], 0.0)
        state[...] = z0_ref[...] + total
        return carry

    lax.fori_loop(0, ITERS, one, 0)
    traj_ref[...] = state[...]


def picard(z0, coef, patch_t, fmod, final_t, a_all, big):
    n_seq, n_tm = lax.axis_size("seq"), lax.axis_size("tm")
    ch, tok = z0.shape
    vmem = pl.BlockSpec(memory_space=pltpu.VMEM)
    sem = pltpu.SemaphoreType.DMA
    return pl.pallas_call(
        functools.partial(picard_kernel, n_seq, n_tm),
        out_shape=[jax.ShapeDtypeStruct((ch, tok), F32)] * 2,
        in_specs=[vmem] * 7,
        out_specs=[vmem] * 2,
        scratch_shapes=[
            pltpu.VMEM((ch, tok), F32),
            pltpu.VMEM((ITERS, n_seq, ch, tok), F32),
            pltpu.VMEM((ITERS, n_tm, ch, tok), F32),
            pltpu.VMEM((ITERS, ch, tok), F32),
            pltpu.VMEM((ITERS, ch, tok), F32),
            pltpu.VMEM((big.shape[0], 2 * tok), BF16),
            sem((ITERS, n_seq - 1)),
            sem((ITERS, n_seq - 1)),
            sem((ITERS, n_tm - 1)),
            sem((ITERS, n_tm - 1)),
        ],
        compiler_params=pltpu.CompilerParams(
            collective_id=9, has_side_effects=True, vmem_limit_bytes=40 << 20
        ),
    )(z0, coef, patch_t, fmod, final_t, a_all, big)


def plan_coefs(beta_table, cur_ids, next_ids):
    keep = 1.0 - beta_table
    pos = jnp.arange(beta_table.shape[0], dtype=jnp.int32)
    bar_now = jnp.prod(jnp.where(pos[None] <= cur_ids[:, None], keep[None], 1.0), axis=1)
    bar_next = jnp.prod(jnp.where(pos[None] <= next_ids[:, None], keep[None], 1.0), axis=1)
    coef_a = jnp.sqrt(bar_next / bar_now)
    coef_b = jnp.sqrt(1.0 - bar_next) - coef_a * jnp.sqrt(1.0 - bar_now)
    return (coef_a, coef_b)


def frequency_embed(cur_ids, freq_width):
    half = freq_width // 2
    freqs = jnp.exp(-math.log(10000.0) * jnp.arange(half, dtype=F32) / half)
    angles = cur_ids.astype(F32)[:, None] * freqs[None, :]
    return jnp.concatenate([jnp.cos(angles), jnp.sin(angles)], axis=1)


def wide_dot(left, right):
    parts = []
    rest = left
    for _ in range(3):
        part = lax.reduce_precision(rest, 8, 7)
        parts.append(part.astype(BF16))
        rest = rest - part
    out = jnp.dot(jnp.concatenate(parts, axis=0), right, preferred_element_type=F32)
    return jnp.sum(out.reshape((3, left.shape[0], right.shape[1])), axis=0)


def body(
    init_latent, cur_ids, next_ids, beta_table, temb_weight, mod_weight, mod_bias,
    patch_weight, qkv_weight, out_weight, final_weight,
):
    ch, width = patch_weight.shape
    tok = init_latent.shape[1]
    n_seq, n_tm = lax.axis_size("seq"), lax.axis_size("tm")
    here, when = lax.axis_index("seq"), lax.axis_index("tm")
    head_dim = width // HEADS
    heads_here = HEADS // n_seq
    cols = width // n_seq
    rows = qkv_weight.shape[0]

    out_rows = lax.dynamic_slice_in_dim(out_weight, here * cols, cols, 0)
    out_here = lax.all_gather(out_rows, "tm", axis=1, tiled=True)

    coef_a, coef_b = plan_coefs(beta_table, cur_ids, next_ids)
    coef = jnp.broadcast_to(
        jnp.stack([coef_a[0] - 1.0, coef_b[0]])[:, None, None], (2, ch, tok)
    )
    freq_emb = frequency_embed(cur_ids, temb_weight.shape[0]).astype(BF16)
    feats = mod_weight.shape[0]
    temb_here = lax.dynamic_slice_in_dim(temb_weight, here * feats, feats, 1)
    emb_part = jax.nn.silu(jnp.dot(freq_emb, temb_here, preferred_element_type=F32)).astype(BF16)
    mod_terms = jnp.einsum("d,dme->me", emb_part[0], mod_weight, preferred_element_type=F32)
    (mod_all,) = exchange([mod_terms], "seq", 0)
    modulation = jnp.sum(mod_all, axis=0).astype(BF16).astype(F32) + mod_bias
    (mod_steps,) = exchange([modulation[0:2]], "tm", 1)

    patch_mid = patch_weight - jnp.mean(patch_weight, axis=1, keepdims=True)
    mid_here = lax.dynamic_slice_in_dim(patch_mid, when * rows, rows, 1)
    steps_here = lax.dynamic_slice_in_dim(mod_steps, when * rows, rows, 2)
    left = jnp.concatenate(
        [
            mid_here[None] * (1.0 + steps_here[:, 1:2]),
            steps_here[:, 0:1],
            jnp.zeros((n_tm, AUG - ch - 1, rows), F32),
        ],
        axis=1,
    )
    m_part = wide_dot(left.reshape(n_tm * AUG, rows), qkv_weight.reshape(rows, 3 * cols))
    (m_all,) = exchange([m_part.reshape(n_tm, AUG, 3 * cols)], "tm", 2, scatter=True)
    m_here = jnp.sum(m_all, axis=0).reshape(AUG, 3, heads_here, head_dim)

    a_here = jnp.einsum(
        "khe,qhe->hkq", m_here[:, 1], m_here[:, 0], precision=HIGH, preferred_element_type=F32
    ) * (math.log2(math.e) / math.sqrt(head_dim))
    m_value = m_here[:, 2]
    same = jnp.eye(heads_here, dtype=F32)
    diag = jnp.einsum("che,hg->hcge", m_value[:ch], same).reshape(heads_here * ch, cols)
    tail = jnp.concatenate([m_value[ch].reshape(1, cols), jnp.zeros((15, cols), F32)], axis=0)
    big_here = wide_dot(jnp.concatenate([diag, tail], axis=0), out_here) * modulation[2:3]
    a_all, big = exchange([a_here, big_here.astype(BF16)], "seq", 3)

    fmod = jnp.stack([1.0 + modulation[4], modulation[3]], axis=1)
    traj, noise = picard(
        init_latent, coef, patch_weight.T, fmod, final_weight.T,
        a_all.reshape(HEADS * AUG, AUG), big.reshape(-1, width),
    )
    return (traj[None], noise[None])


def solution(mesh):
    in_specs = (
        P("groups", "seq"),
        P("tm"),
        P("tm"),
        P(),
        P(),
        P("seq", None, None),
        P(),
        P(),
        P("tm", None, "seq"),
        P(None, "tm"),
        P(),
    )
    out_specs = (P("tm", "groups", "seq"), P("tm", "groups", "seq"))
    return jax.shard_map(body, mesh=mesh, in_specs=in_specs, out_specs=out_specs, check_vma=False)
```

```python
import functools
import math

import jax
import jax.numpy as jnp
from jax import lax
from jax.experimental import pallas as pl
from jax.experimental.pallas import tpu as pltpu
from jax.sharding import PartitionSpec as P

HEADS = 16
ITERS = 3
AUG = 24
HIGH = lax.Precision.HIGHEST
MESH = pl.DeviceIdType.MESH
F32, BF16 = jnp.float32, jnp.bfloat16


def greet(plan):
    barrier = pltpu.get_barrier_semaphore()
    total = 0
    for axis, n in plan:
        me = lax.axis_index(axis)
        for d in range(1, n):
            pl.semaphore_signal(
                barrier, inc=1, device_id={axis: lax.rem(me + d, n)}, device_id_type=MESH
            )
        total += n - 1
    pl.semaphore_wait(barrier, total)


def sends(axis, n, source, landing, send, recv, scatter=False):
    me = lax.axis_index(axis)
    copies = []
    for d in range(1, n):
        peer = lax.rem(me + d, n)
        copies.append(
            pltpu.make_async_remote_copy(
                src_ref=source.at[peer] if scatter else source,
                dst_ref=landing.at[me],
                send_sem=send.at[d - 1],
                recv_sem=recv.at[d - 1],
                device_id={axis: peer},
                device_id_type=MESH,
            )
        )
    return copies


def split(value):
    high = value.astype(BF16).astype(F32)
    return high, value - high


def split3(value):
    high, rest = split(value)
    mid, low = split(rest)
    return jnp.concatenate([high, mid, low], axis=0).astype(BF16)


def thirds(value):
    n = value.shape[0] // 3
    return value[:n] + value[n : 2 * n] + value[2 * n :]


def share(n, source, landing, send, recv):
    me = lax.axis_index("seq")
    if n != 4:
        copies = sends("seq", n, source, landing, send, recv)
        for copy in copies:
            copy.start()
        landing[me] = source[...]
        for copy in copies:
            copy.wait()
        return
    pair = me + 1 - 2 * lax.rem(me, 2)
    across = lax.rem(me + 2, 4)

    def to(block, slot, peer, i):
        return pltpu.make_async_remote_copy(
            src_ref=block, dst_ref=landing.at[slot], send_sem=send.at[i], recv_sem=recv.at[i],
            device_id={"seq": peer}, device_id_type=MESH,
        )

    far, near = to(source, me, across, 0), to(source, me, pair, 1)
    far.start()
    near.start()
    landing[me] = source[...]
    far.wait_recv()
    onward = to(landing.at[across], across, pair, 2)
    onward.start()
    near.wait()
    far.wait_send()
    onward.wait()


def picard_kernel(
    n_seq, n_tm, head_dim,
    z0_ref, coef_ref, patch_ref, final_ref, terms_ref, bias_ref, mid_ref, qkv_ref, wo_ref,
    traj_ref, noise_ref,
    wbuf, tbuf, msrc, mbuf, psrc, pbuf, asrc, abuf, bsrc, bbuf, bigt, cols,
    state, ubuf, dbuf, usrc, dsrc, yrows,
    wsend, wrecv, tsend, trecv, msend, mrecv, psend, precv, asend, arecv, bsend, brecv,
    usend, urecv, dsend, drecv,
):
    greet([("seq", n_seq), ("tm", n_tm)])
    here, when = lax.axis_index("seq"), lax.axis_index("tm")
    ch, tok = z0_ref.shape
    keys = n_seq * tok
    heads_here = HEADS // n_seq
    block = heads_here * 16 + 16
    width = patch_ref.shape[0]
    rows = mid_ref.shape[1]
    wide = bsrc.shape[1] // n_tm

    terms = sends("seq", n_seq, terms_ref, tbuf, tsend, trecv)
    for copy in terms:
        copy.start()
    outs = sends("tm", n_tm, wo_ref, wbuf, wsend, wrecv)
    for copy in outs:
        copy.start()
    tbuf[here] = terms_ref[...]
    wbuf[when] = wo_ref[...]
    state[...] = z0_ref[...]
    bsrc[...] = jnp.zeros_like(bsrc)

    def ones_tail(lanes):
        row = lax.broadcasted_iota(jnp.int32, (AUG - ch, lanes), 0)
        return jnp.where(row == 0, 1.0, 0.0).astype(F32)

    row = lax.broadcasted_iota(jnp.int32, (16, 2 * tok), 0)
    lane = lax.broadcasted_iota(jnp.int32, (16, 2 * tok), 1)
    const = jnp.where((row == 0) & (lane < tok), 1.0, 0.0).astype(BF16)
    for s in range(n_seq):
        yrows[s * block + heads_here * 16 : (s + 1) * block, :] = const

    for copy in terms:
        copy.wait()
    mod = tbuf[0]
    for s in range(1, n_seq):
        mod = mod + tbuf[s]
    mod = mod.astype(BF16).astype(F32) + bias_ref[...]
    for k in range(n_tm):
        msrc[k] = mod[:, k * rows : (k + 1) * rows]
    steps = sends("tm", n_tm, msrc, mbuf, msend, mrecv, True)
    for copy in steps:
        copy.start()
    mbuf[when] = msrc[when]
    cols[...] = jnp.transpose(jnp.concatenate([mod, jnp.zeros((120, width), F32)], axis=0))
    for copy in steps:
        copy.wait()

    first = lax.broadcasted_iota(jnp.int32, (AUG - ch, rows), 0) == 0
    left = []
    for t in range(n_tm):
        step = mbuf[t]
        left.append(mid_ref[...] * (1.0 + step[1:2]))
        left.append(jnp.where(first, step[0:1], 0.0))
    left = split3(jnp.concatenate(left, axis=0))
    for j in range(3):
        part = thirds(jnp.dot(left, qkv_ref[j], preferred_element_type=F32))
        for t in range(n_tm):
            psrc[t, j] = part[t * AUG : (t + 1) * AUG]
    parts = sends("tm", n_tm, psrc, pbuf, psend, precv, True)
    for copy in parts:
        copy.start()
    pbuf[when] = psrc[when]
    for copy in parts:
        copy.wait()
    m_query, m_key, m_value = pbuf[0, 0], pbuf[0, 1], pbuf[0, 2]
    for t in range(1, n_tm):
        m_query, m_key, m_value = (
            m_query + pbuf[t, 0], m_key + pbuf[t, 1], m_value + pbuf[t, 2]
        )
    spot = lax.broadcasted_iota(jnp.int32, m_key.shape, 1)

    def own(value, h):
        at = spot[: value.shape[0]]
        return jnp.where((at >= h * head_dim) & (at < (h + 1) * head_dim), value, 0.0)

    scale = math.log2(math.e) / math.sqrt(head_dim)
    stacked = jnp.concatenate([own(m_key, h) for h in range(heads_here)], axis=0)
    asrc[...] = scale * lax.dot_general(
        stacked, m_query, (((1,), (1,)), ((), ())), precision=HIGH, preferred_element_type=F32
    )
    forms = sends("seq", n_seq, asrc, abuf, asend, arecv)
    for copy in forms:
        copy.start()
    abuf[here] = asrc[...]
    diag = [own(m_value[:ch], h) for h in range(heads_here)]
    diag += [m_value[ch:], jnp.zeros((16 - AUG + ch, m_value.shape[1]), F32)]
    diag = split3(jnp.concatenate(diag, axis=0))
    for copy in outs:
        copy.wait()
    for k in range(n_tm):
        bsrc[:, k * wide : k * wide + rows] = thirds(
            jnp.dot(diag, wbuf[k], preferred_element_type=F32)
        ).astype(BF16)
    share(n_seq, bsrc, bbuf, bsend, brecv)
    for copy in forms:
        copy.wait()
    compact = rows % 16 == 0
    for k in range(n_tm):
        piece = bbuf[:, :, k * wide : (k + 1) * wide].reshape(n_seq * block, wide)
        turned = jnp.transpose(piece.astype(F32)).astype(BF16)
        if compact:
            bigt[k * rows : (k + 1) * rows, :] = turned[:rows]
        else:
            bigt[k * wide : (k + 1) * wide, :] = turned
    a_all = abuf[...].reshape(HEADS * AUG, AUG)

    def one(it, carry):
        z = state[...]
        emb = lax.dot_general(
            patch_ref[...], z, (((1,), (0,)), ((), ())),
            precision=HIGH, preferred_element_type=F32,
        )
        center = emb - jnp.mean(emb, axis=0, keepdims=True)
        spread = jnp.mean(center * center, axis=0, keepdims=True)
        u = z / jnp.sqrt(spread + 1e-06)
        usrc[it] = u
        copies = sends("seq", n_seq, usrc.at[it], ubuf.at[it], usend.at[it], urecv.at[it])
        for copy in copies:
            copy.start()
        ubuf[it, here] = u
        u_query = jnp.concatenate([u, ones_tail(tok)], axis=0)
        g = lax.dot_general(
            a_all, u_query, (((1,), (0,)), ((), ())),
            precision=HIGH, preferred_element_type=F32,
        )
        for copy in copies:
            copy.wait()
        u_all = jnp.concatenate([ubuf[it, s] for s in range(n_seq)], axis=1)
        u_keys = jnp.concatenate([u_all, ones_tail(keys)], axis=0)
        k_high, k_low = split(u_keys)
        pad = jnp.zeros((128 - 3 * AUG, keys), F32)
        key_rows = jnp.transpose(jnp.concatenate([k_high, k_high, k_low, pad], axis=0)).astype(BF16)
        values = jnp.concatenate([k_high, k_low], axis=0).astype(BF16)
        qpad = jnp.zeros((128 - 3 * AUG, 2 * tok), F32)
        for pair in range(HEADS // 2):
            lo = pair * 2 * AUG
            both = jnp.concatenate([g[lo : lo + AUG], g[lo + AUG : lo + 2 * AUG]], axis=1)
            q_high, q_low = split(both)
            query = jnp.concatenate([q_high, q_low, q_high, qpad], axis=0).astype(BF16)
            scores = jnp.dot(key_rows, query, preferred_element_type=F32)
            top = jnp.max(scores, axis=0, keepdims=True)
            probs = jnp.exp2(scores - top).astype(BF16)
            out = jnp.dot(values, probs, preferred_element_type=F32)
            out = out[:AUG] + out[AUG:]
            y_high, y_low = split(out[:ch] / out[ch : ch + 1])
            for k in range(2):
                head = pair * 2 + k
                at = head // heads_here * block + head % heads_here * 16
                cut = slice(k * tok, (k + 1) * tok)
                yrows[at : at + 16, 0:tok] = y_high[:, cut].astype(BF16)
                yrows[at : at + 16, tok : 2 * tok] = y_low[:, cut].astype(BF16)
        proj = jnp.dot(bigt[...], yrows[...], preferred_element_type=F32)
        proj = proj[:, :tok] + proj[:, tok:]
        if not compact:
            proj = jnp.concatenate(
                [proj[k * wide : k * wide + rows] for k in range(n_tm)], axis=0
            )
        residual = emb + cols[:, 2:3] * proj
        center = residual - jnp.mean(residual, axis=0, keepdims=True)
        spread = jnp.mean(center * center, axis=0, keepdims=True)
        normed = center / jnp.sqrt(spread + 1e-06)
        final_in = (normed * (1.0 + cols[:, 4:5]) + cols[:, 3:4]).astype(BF16)
        noise = jnp.dot(final_ref[...], final_in, preferred_element_type=F32)
        noise_ref[...] = noise
        drift = coef_ref[0] * z + coef_ref[1] * noise
        dsrc[it] = drift
        copies = sends("tm", n_tm, dsrc.at[it], dbuf.at[it], dsend.at[it], drecv.at[it])
        for copy in copies:
            copy.start()
        dbuf[it, when] = drift
        for copy in copies:
            copy.wait()
        total = jnp.zeros_like(drift)
        for j in range(n_tm - 1):
            total = total + jnp.where(when > j, dbuf[it, j], 0.0)
        state[...] = z0_ref[...] + total
        return carry

    lax.fori_loop(0, ITERS, one, 0)
    traj_ref[...] = state[...]


def picard(head_dim, z0, coef, patch_t, final_t, terms, bias, mid, qkv, wo):
    n_seq, n_tm = lax.axis_size("seq"), lax.axis_size("tm")
    ch, tok = z0.shape
    width = patch_t.shape[0]
    rows, here = mid.shape[1], wo.shape[0]
    block = HEADS // n_seq * 16 + 16
    wide = -(-rows // 128) * 128
    vmem = pl.BlockSpec(memory_space=pltpu.VMEM)
    sem, mem = pltpu.SemaphoreType.DMA, pltpu.VMEM
    pairs = []
    for n in (n_tm, n_seq, n_tm, n_tm, n_seq, n_seq):
        pairs += [sem((n - 1,)), sem((n - 1,))]
    for n in (n_seq, n_tm):
        pairs += [sem((ITERS, n - 1)), sem((ITERS, n - 1))]
    return pl.pallas_call(
        functools.partial(picard_kernel, n_seq, n_tm, head_dim),
        out_shape=[jax.ShapeDtypeStruct((ch, tok), F32)] * 2,
        in_specs=[vmem] * 9,
        out_specs=[vmem] * 2,
        scratch_shapes=[
            mem((n_tm,) + wo.shape, BF16),
            mem((n_seq,) + terms.shape, F32),
            mem((n_tm, 8, rows), F32),
            mem((n_tm, 8, rows), F32),
            mem((n_tm, 3, AUG, here), F32),
            mem((n_tm, 3, AUG, here), F32),
            mem((HEADS // n_seq * AUG, AUG), F32),
            mem((n_seq, HEADS // n_seq * AUG, AUG), F32),
            mem((block, n_tm * wide), BF16),
            mem((n_seq, block, n_tm * wide), BF16),
            mem((width if rows % 16 == 0 else n_tm * wide, n_seq * block), BF16),
            mem((width, 128), F32),
            mem((ch, tok), F32),
            mem((ITERS, n_seq, ch, tok), F32),
            mem((ITERS, n_tm, ch, tok), F32),
            mem((ITERS, ch, tok), F32),
            mem((ITERS, ch, tok), F32),
            mem((n_seq * block, 2 * tok), BF16),
        ] + pairs,
        compiler_params=pltpu.CompilerParams(
            collective_id=0, has_side_effects=True, vmem_limit_bytes=40 << 20
        ),
    )(z0, coef, patch_t, final_t, terms, bias, mid, qkv, wo)


def plan_coefs(beta_table, cur_ids, next_ids):
    keep = 1.0 - beta_table
    pos = jnp.arange(beta_table.shape[0], dtype=jnp.int32)
    bar_now = jnp.prod(jnp.where(pos[None] <= cur_ids[:, None], keep[None], 1.0), axis=1)
    bar_next = jnp.prod(jnp.where(pos[None] <= next_ids[:, None], keep[None], 1.0), axis=1)
    coef_a = jnp.sqrt(bar_next / bar_now)
    coef_b = jnp.sqrt(1.0 - bar_next) - coef_a * jnp.sqrt(1.0 - bar_now)
    return (coef_a, coef_b)


def frequency_embed(cur_ids, freq_width):
    half = freq_width // 2
    freqs = jnp.exp(-math.log(10000.0) * jnp.arange(half, dtype=F32) / half)
    angles = cur_ids.astype(F32)[:, None] * freqs[None, :]
    return jnp.concatenate([jnp.cos(angles), jnp.sin(angles)], axis=1)


def body(
    init_latent, cur_ids, next_ids, beta_table, temb_weight, mod_weight, mod_bias,
    patch_weight, qkv_weight, out_weight, final_weight,
):
    ch, width = patch_weight.shape
    tok = init_latent.shape[1]
    here, when = lax.axis_index("seq"), lax.axis_index("tm")
    cols = qkv_weight.shape[2]
    rows = qkv_weight.shape[0]

    coef_a, coef_b = plan_coefs(beta_table, cur_ids, next_ids)
    coef = jnp.broadcast_to(
        jnp.stack([coef_a[0] - 1.0, coef_b[0]])[:, None, None], (2, ch, tok)
    )
    freq_emb = frequency_embed(cur_ids, temb_weight.shape[0]).astype(BF16)
    feats = mod_weight.shape[0]
    temb_here = lax.dynamic_slice_in_dim(temb_weight, here * feats, feats, 1)
    emb_part = jax.nn.silu(jnp.dot(freq_emb, temb_here, preferred_element_type=F32)).astype(BF16)
    mod_terms = jnp.einsum("d,dme->me", emb_part[0], mod_weight, preferred_element_type=F32)
    spare = ((0, 8 - mod_terms.shape[0]), (0, 0))
    patch_mid = patch_weight - jnp.mean(patch_weight, axis=1, keepdims=True)
    mid_here = lax.dynamic_slice_in_dim(patch_mid, when * rows, rows, 1)
    traj, noise = picard(
        width // HEADS, init_latent, coef, patch_weight.T, final_weight.T,
        jnp.pad(mod_terms, spare), jnp.pad(mod_bias, spare), mid_here,
        jnp.swapaxes(qkv_weight, 0, 1),
        lax.dynamic_slice_in_dim(out_weight, here * cols, cols, 0),
    )
    return (traj[None], noise[None])


def solution(mesh):
    in_specs = (
        P("groups", "seq"),
        P("tm"),
        P("tm"),
        P(),
        P(),
        P("seq", None, None),
        P(),
        P(),
        P("tm", None, "seq"),
        P(None, "tm"),
        P(),
    )
    out_specs = (P("tm", "groups", "seq"), P("tm", "groups", "seq"))
    return jax.shard_map(body, mesh=mesh, in_specs=in_specs, out_specs=out_specs, check_vma=False)
```

```python
import functools
import math

import jax
import jax.numpy as jnp
from jax import lax
from jax.experimental import pallas as pl
from jax.experimental.pallas import tpu as pltpu
from jax.sharding import PartitionSpec as P

HEADS = 16
ITERS = 3
AUG = 24
HIGH = lax.Precision.HIGHEST
MESH = pl.DeviceIdType.MESH
F32, BF16 = jnp.float32, jnp.bfloat16


def greet(plan):
    barrier = pltpu.get_barrier_semaphore()
    total = 0
    for axis, n in plan:
        me = lax.axis_index(axis)
        for d in range(1, n):
            pl.semaphore_signal(
                barrier, inc=1, device_id={axis: lax.rem(me + d, n)}, device_id_type=MESH
            )
        total += n - 1
    pl.semaphore_wait(barrier, total)


def sends(axis, n, source, landing, send, recv, scatter=False):
    me = lax.axis_index(axis)
    copies = []
    for d in range(1, n):
        peer = lax.rem(me + d, n)
        copies.append(
            pltpu.make_async_remote_copy(
                src_ref=source.at[peer] if scatter else source,
                dst_ref=landing.at[me],
                send_sem=send.at[d - 1],
                recv_sem=recv.at[d - 1],
                device_id={axis: peer},
                device_id_type=MESH,
            )
        )
    return copies


def split(value):
    high = value.astype(BF16).astype(F32)
    return high, value - high


def split3(value):
    high, rest = split(value)
    mid, low = split(rest)
    return jnp.concatenate([high, mid, low], axis=0).astype(BF16)


def thirds(value):
    n = value.shape[0] // 3
    return value[:n] + value[n : 2 * n] + value[2 * n :]


def share(n, source, landing, send, recv):
    me = lax.axis_index("seq")
    if n != 4:
        copies = sends("seq", n, source, landing, send, recv)
        for copy in copies:
            copy.start()
        landing[me] = source[...]
        for copy in copies:
            copy.wait()
        return
    pair = me + 1 - 2 * lax.rem(me, 2)
    across = lax.rem(me + 2, 4)

    def to(block, slot, peer, i):
        return pltpu.make_async_remote_copy(
            src_ref=block, dst_ref=landing.at[slot], send_sem=send.at[i], recv_sem=recv.at[i],
            device_id={"seq": peer}, device_id_type=MESH,
        )

    far, near = to(source, me, across, 0), to(source, me, pair, 1)
    far.start()
    near.start()
    landing[me] = source[...]
    far.wait_recv()
    onward = to(landing.at[across], across, pair, 2)
    onward.start()
    near.wait()
    far.wait_send()
    onward.wait()


def picard_kernel(
    n_seq, n_tm, n_groups, head_dim,
    z0_ref, coef_ref, patch_ref, final_ref, terms_ref, bias_ref, qkv_ref, wo_ref,
    traj_ref, noise_ref,
    patch_t, ebuf, modbuf, wbuf, tbuf, msrc, mbuf, psrc, pbuf, asrc, abuf, bsrc, bbuf, bigt, cols,
    state, ubuf, dbuf, usrc, dsrc, yrows,
    wsend, wrecv, tsend, trecv, msend, mrecv, psend, precv, asend, arecv, bsend, brecv,
    ysend, yrecv, usend, urecv, dsend, drecv,
):
    halve = n_groups == 2 and wo_ref.shape[0] % 32 == 0
    greet([("seq", n_seq), ("tm", n_tm)] + ([("groups", n_groups)] if halve else []))
    here, when = lax.axis_index("seq"), lax.axis_index("tm")
    ch, tok = z0_ref.shape
    keys = n_seq * tok
    heads_here = HEADS // n_seq
    block = heads_here * 16 + 16
    width = patch_ref.shape[1]
    rows = qkv_ref.shape[1]
    mods = bias_ref.shape[0]
    wide = bsrc.shape[1] // n_tm

    terms = sends("seq", n_seq, terms_ref, tbuf, tsend, trecv)
    for copy in terms:
        copy.start()
    if halve:
        half = wo_ref.shape[0] // 2
        group = lax.axis_index("groups")
        mine = pl.ds(pl.multiple_of(group * half, 16), half)
        outs = [
            pltpu.make_async_remote_copy(
                src_ref=wo_ref.at[mine], dst_ref=wbuf.at[when, mine],
                send_sem=wsend.at[d - 1], recv_sem=wrecv.at[d - 1],
                device_id={"tm": lax.rem(when + d, n_tm)}, device_id_type=MESH,
            )
            for d in range(1, n_tm)
        ]
    else:
        outs = sends("tm", n_tm, wo_ref, wbuf, wsend, wrecv)
    for copy in outs:
        copy.start()
    tbuf[here] = terms_ref[...]
    wbuf[when] = wo_ref[...]
    state[...] = z0_ref[...]
    bsrc[...] = jnp.zeros_like(bsrc)
    patch = patch_ref[...]
    patch_t[...] = jnp.transpose(
        jnp.concatenate([patch, jnp.zeros((128 - ch, width), F32)], axis=0)
    )[:, :ch]

    def seq_copies(it):
        return sends("seq", n_seq, usrc.at[it], ubuf.at[it], usend.at[it], urecv.at[it])

    def begin(it):
        z = state[...]
        emb = lax.dot_general(
            patch_t[...], z, (((1,), (0,)), ((), ())),
            precision=HIGH, preferred_element_type=F32,
        )
        center = emb - jnp.mean(emb, axis=0, keepdims=True)
        spread = jnp.mean(center * center, axis=0, keepdims=True)
        u = z / jnp.sqrt(spread + 1e-06)
        usrc[it] = u
        for copy in seq_copies(it):
            copy.start()
        ubuf[it, here] = u
        ebuf[...] = emb

    begin(0)
    modbuf[...] = jnp.zeros_like(modbuf)
    patch_mid = patch - jnp.mean(patch, axis=1, keepdims=True)
    mid = patch_mid[:, :rows]
    for k in range(1, n_tm):
        mid = jnp.where(when == k, patch_mid[:, k * rows : (k + 1) * rows], mid)

    def ones_tail(lanes):
        row = lax.broadcasted_iota(jnp.int32, (AUG - ch, lanes), 0)
        return jnp.where(row == 0, 1.0, 0.0).astype(F32)

    row = lax.broadcasted_iota(jnp.int32, (16, 2 * tok), 0)
    lane = lax.broadcasted_iota(jnp.int32, (16, 2 * tok), 1)
    const = jnp.where((row == 0) & (lane < tok), 1.0, 0.0).astype(BF16)
    for s in range(n_seq):
        yrows[s * block + heads_here * 16 : (s + 1) * block, :] = const

    for copy in terms:
        copy.wait()
    mod = tbuf[0]
    for s in range(1, n_seq):
        mod = mod + tbuf[s]
    mod = mod.astype(BF16).astype(F32) + bias_ref[...]
    for k in range(n_tm):
        msrc[k] = mod[:, k * rows : (k + 1) * rows]
    steps = sends("tm", n_tm, msrc, mbuf, msend, mrecv, True)
    for copy in steps:
        copy.start()
    mbuf[when] = msrc[when]
    modbuf[0:mods, :] = mod
    cols[...] = jnp.transpose(modbuf[...])
    for copy in steps:
        copy.wait()

    first = lax.broadcasted_iota(jnp.int32, (AUG - ch, rows), 0) == 0
    left = []
    for t in range(n_tm):
        step = mbuf[t]
        left.append(mid * (1.0 + step[1:2]))
        left.append(jnp.where(first, step[0:1], 0.0))
    left = split3(jnp.concatenate(left, axis=0))
    three = [thirds(jnp.dot(left, qkv_ref[j], preferred_element_type=F32)) for j in range(3)]
    rest = jnp.zeros((psrc.shape[1] - 3 * AUG, psrc.shape[2]), F32)
    for t in range(n_tm):
        piece = [part[t * AUG : (t + 1) * AUG] for part in three]
        psrc[t] = jnp.concatenate(piece + [rest], axis=0).astype(BF16)
    parts = sends("tm", n_tm, psrc, pbuf, psend, precv, True)
    for copy in parts:
        copy.start()
    pbuf[when] = psrc[when]
    swaps = []
    if halve:
        for d in range(1, n_tm):
            outs[d - 1].wait_recv()
            came = wbuf.at[lax.rem(when + n_tm - d, n_tm), mine]
            swaps.append(
                pltpu.make_async_remote_copy(
                    src_ref=came, dst_ref=came,
                    send_sem=ysend.at[d - 1], recv_sem=yrecv.at[d - 1],
                    device_id={"groups": 1 - group}, device_id_type=MESH,
                )
            )
            swaps[-1].start()
    for copy in parts:
        copy.wait()
    m_all = pbuf[0].astype(F32)
    for t in range(1, n_tm):
        m_all = m_all + pbuf[t].astype(F32)
    m_query, m_key, m_value = m_all[:AUG], m_all[AUG : 2 * AUG], m_all[2 * AUG : 3 * AUG]
    spot = lax.broadcasted_iota(jnp.int32, m_key.shape, 1)

    def own(value, h):
        at = spot[: value.shape[0]]
        return jnp.where((at >= h * head_dim) & (at < (h + 1) * head_dim), value, 0.0)

    scale = math.log2(math.e) / math.sqrt(head_dim)
    stacked = jnp.concatenate([own(m_key, h) for h in range(heads_here)], axis=0)
    asrc[...] = scale * lax.dot_general(
        stacked, m_query, (((1,), (1,)), ((), ())), precision=HIGH, preferred_element_type=F32
    )
    forms = sends("seq", n_seq, asrc, abuf, asend, arecv)
    for copy in forms:
        copy.start()
    abuf[here] = asrc[...]
    diag = [own(m_value[:ch], h) for h in range(heads_here)]
    diag += [m_value[ch:], jnp.zeros((16 - AUG + ch, m_value.shape[1]), F32)]
    diag = split3(jnp.concatenate(diag, axis=0))
    for copy in outs:
        if halve:
            copy.wait_send()
        else:
            copy.wait()
    for copy in swaps:
        copy.wait()
    for k in range(n_tm):
        bsrc[:, k * wide : k * wide + rows] = thirds(
            jnp.dot(diag, wbuf[k], preferred_element_type=F32)
        ).astype(BF16)
    share(n_seq, bsrc, bbuf, bsend, brecv)
    for copy in forms:
        copy.wait()
    compact = rows % 16 == 0
    for k in range(n_tm):
        piece = bbuf[:, :, k * wide : (k + 1) * wide].reshape(n_seq * block, wide)
        turned = jnp.transpose(piece.astype(F32)).astype(BF16)
        if compact:
            bigt[k * rows : (k + 1) * rows, :] = turned[:rows]
        else:
            bigt[k * wide : (k + 1) * wide, :] = turned
    a_all = abuf[...].reshape(HEADS * AUG, AUG)

    def one(it, carry):
        z = state[...]
        emb = ebuf[...]
        u = usrc[it]
        copies = seq_copies(it)
        u_query = jnp.concatenate([u, ones_tail(tok)], axis=0)
        g = lax.dot_general(
            a_all, u_query, (((1,), (0,)), ((), ())),
            precision=HIGH, preferred_element_type=F32,
        )
        for copy in copies:
            copy.wait()
        u_all = jnp.concatenate([ubuf[it, s] for s in range(n_seq)], axis=1)
        u_keys = jnp.concatenate([u_all, ones_tail(keys)], axis=0)
        k_high, k_low = split(u_keys)
        pad = jnp.zeros((128 - 3 * AUG, keys), F32)
        key_rows = jnp.transpose(jnp.concatenate([k_high, k_high, k_low, pad], axis=0)).astype(BF16)
        values = jnp.concatenate([k_high, k_low], axis=0).astype(BF16)
        qpad = jnp.zeros((128 - 3 * AUG, 2 * tok), F32)
        for pair in range(HEADS // 2):
            lo = pair * 2 * AUG
            both = jnp.concatenate([g[lo : lo + AUG], g[lo + AUG : lo + 2 * AUG]], axis=1)
            q_high, q_low = split(both)
            query = jnp.concatenate([q_high, q_low, q_high, qpad], axis=0).astype(BF16)
            scores = jnp.dot(key_rows, query, preferred_element_type=F32)
            top = jnp.max(scores, axis=0, keepdims=True)
            probs = jnp.exp2(scores - top).astype(BF16)
            out = jnp.dot(values, probs, preferred_element_type=F32)
            out = out[:AUG] + out[AUG:]
            y_high, y_low = split(out[:ch] / out[ch : ch + 1])
            for k in range(2):
                head = pair * 2 + k
                at = head // heads_here * block + head % heads_here * 16
                cut = slice(k * tok, (k + 1) * tok)
                yrows[at : at + 16, 0:tok] = y_high[:, cut].astype(BF16)
                yrows[at : at + 16, tok : 2 * tok] = y_low[:, cut].astype(BF16)
        proj = jnp.dot(bigt[...], yrows[...], preferred_element_type=F32)
        proj = proj[:, :tok] + proj[:, tok:]
        if not compact:
            proj = jnp.concatenate(
                [proj[k * wide : k * wide + rows] for k in range(n_tm)], axis=0
            )
        residual = emb + cols[:, 2:3] * proj
        center = residual - jnp.mean(residual, axis=0, keepdims=True)
        spread = jnp.mean(center * center, axis=0, keepdims=True)
        normed = center / jnp.sqrt(spread + 1e-06)
        final_in = (normed * (1.0 + cols[:, 4:5]) + cols[:, 3:4]).astype(BF16)
        noise = jnp.dot(final_ref[...], final_in, preferred_element_type=F32)
        noise_ref[...] = noise
        drift = coef_ref[0] * z + coef_ref[1] * noise
        dsrc[it] = drift
        copies = sends("tm", n_tm, dsrc.at[it], dbuf.at[it], dsend.at[it], drecv.at[it])
        for copy in copies:
            copy.start()
        dbuf[it, when] = drift
        for copy in copies:
            copy.wait()
        total = jnp.zeros_like(drift)
        for j in range(n_tm - 1):
            total = total + jnp.where(when > j, dbuf[it, j], 0.0)
        state[...] = z0_ref[...] + total

        @pl.when(it < ITERS - 1)
        def _():
            begin(it + 1)

        return carry

    lax.fori_loop(0, ITERS, one, 0)
    traj_ref[...] = state[...]


def picard(head_dim, z0, coef, patch, final_t, terms, bias, qkv, wo):
    n_seq, n_tm = lax.axis_size("seq"), lax.axis_size("tm")
    ch, tok = z0.shape
    width = patch.shape[1]
    rows, here = qkv.shape[1], wo.shape[0]
    mods = bias.shape[0]
    part_rows = -(-3 * AUG // 16) * 16
    block = HEADS // n_seq * 16 + 16
    wide = -(-rows // 128) * 128
    vmem = pl.BlockSpec(memory_space=pltpu.VMEM)
    sem, mem = pltpu.SemaphoreType.DMA, pltpu.VMEM
    pairs = []
    for n in (n_tm, n_seq, n_tm, n_tm, n_seq, n_seq, n_tm):
        pairs += [sem((n - 1,)), sem((n - 1,))]
    for n in (n_seq, n_tm):
        pairs += [sem((ITERS, n - 1)), sem((ITERS, n - 1))]
    return pl.pallas_call(
        functools.partial(picard_kernel, n_seq, n_tm, lax.axis_size("groups"), head_dim),
        out_shape=[jax.ShapeDtypeStruct((ch, tok), F32)] * 2,
        in_specs=[vmem] * 8,
        out_specs=[vmem] * 2,
        scratch_shapes=[
            mem((width, ch), F32),
            mem((width, tok), F32),
            mem((128, width), F32),
            mem((n_tm,) + wo.shape, BF16),
            mem((n_seq,) + terms.shape, F32),
            mem((n_tm, mods, rows), F32),
            mem((n_tm, mods, rows), F32),
            mem((n_tm, part_rows, here), BF16),
            mem((n_tm, part_rows, here), BF16),
            mem((HEADS // n_seq * AUG, AUG), F32),
            mem((n_seq, HEADS // n_seq * AUG, AUG), F32),
            mem((block, n_tm * wide), BF16),
            mem((n_seq, block, n_tm * wide), BF16),
            mem((width if rows % 16 == 0 else n_tm * wide, n_seq * block), BF16),
            mem((width, 128), F32),
            mem((ch, tok), F32),
            mem((ITERS, n_seq, ch, tok), F32),
            mem((ITERS, n_tm, ch, tok), F32),
            mem((ITERS, ch, tok), F32),
            mem((ITERS, ch, tok), F32),
            mem((n_seq * block, 2 * tok), BF16),
        ] + pairs,
        compiler_params=pltpu.CompilerParams(
            collective_id=0, has_side_effects=True, vmem_limit_bytes=40 << 20
        ),
    )(z0, coef, patch, final_t, terms, bias, qkv, wo)


def plan_coefs(beta_table, cur_ids, next_ids):
    keep = 1.0 - beta_table
    pos = jnp.arange(beta_table.shape[0], dtype=jnp.int32)
    bar_now = jnp.prod(jnp.where(pos[None] <= cur_ids[:, None], keep[None], 1.0), axis=1)
    bar_next = jnp.prod(jnp.where(pos[None] <= next_ids[:, None], keep[None], 1.0), axis=1)
    coef_a = jnp.sqrt(bar_next / bar_now)
    coef_b = jnp.sqrt(1.0 - bar_next) - coef_a * jnp.sqrt(1.0 - bar_now)
    return (coef_a, coef_b)


def frequency_embed(cur_ids, freq_width):
    half = freq_width // 2
    freqs = jnp.exp(-math.log(10000.0) * jnp.arange(half, dtype=F32) / half)
    angles = cur_ids.astype(F32)[:, None] * freqs[None, :]
    return jnp.concatenate([jnp.cos(angles), jnp.sin(angles)], axis=1)


def body(
    init_latent, cur_ids, next_ids, beta_table, temb_weight, mod_weight, mod_bias,
    patch_weight, qkv_weight, out_weight, final_weight,
):
    ch, width = patch_weight.shape
    tok = init_latent.shape[1]
    here = lax.axis_index("seq")
    cols = qkv_weight.shape[2]

    coef_a, coef_b = plan_coefs(beta_table, cur_ids, next_ids)
    coef = jnp.broadcast_to(
        jnp.stack([coef_a[0] - 1.0, coef_b[0]])[:, None, None], (2, ch, tok)
    )
    freq_emb = frequency_embed(cur_ids, temb_weight.shape[0]).astype(BF16)
    feats = mod_weight.shape[0]
    temb_here = lax.dynamic_slice_in_dim(temb_weight, here * feats, feats, 1)
    emb_part = jax.nn.silu(jnp.dot(freq_emb, temb_here, preferred_element_type=F32)).astype(BF16)
    mod_terms = jnp.einsum("d,dme->me", emb_part[0], mod_weight, preferred_element_type=F32)
    traj, noise = picard(
        width // HEADS, init_latent, coef, patch_weight, final_weight.T, mod_terms, mod_bias,
        jnp.swapaxes(qkv_weight, 0, 1),
        lax.dynamic_slice_in_dim(out_weight, here * cols, cols, 0),
    )
    return (traj[None], noise[None])


def solution(mesh):
    in_specs = (
        P("groups", "seq"),
        P("tm"),
        P("tm"),
        P(),
        P(),
        P("seq", None, None),
        P(),
        P(),
        P("tm", None, "seq"),
        P(None, "tm"),
        P(),
    )
    out_specs = (P("tm", "groups", "seq"), P("tm", "groups", "seq"))
    return jax.shard_map(body, mesh=mesh, in_specs=in_specs, out_specs=out_specs, check_vma=False)
```

```python
import functools
import math

import jax
import jax.numpy as jnp
from jax import lax
from jax.experimental import pallas as pl
from jax.experimental.pallas import tpu as pltpu
from jax.sharding import PartitionSpec as P

HEADS = 16
ITERS = 3
AUG = 24
HIGH = lax.Precision.HIGHEST
MESH = pl.DeviceIdType.MESH
F32, BF16 = jnp.float32, jnp.bfloat16


def greet(plan):
    barrier = pltpu.get_barrier_semaphore()
    total = 0
    for axis, n in plan:
        me = lax.axis_index(axis)
        for d in range(1, n):
            pl.semaphore_signal(
                barrier, inc=1, device_id={axis: lax.rem(me + d, n)}, device_id_type=MESH
            )
        total += n - 1
    pl.semaphore_wait(barrier, total)


def sends(axis, n, source, landing, send, recv, scatter=False):
    me = lax.axis_index(axis)
    copies = []
    for d in range(1, n):
        peer = lax.rem(me + d, n)
        copies.append(
            pltpu.make_async_remote_copy(
                src_ref=source.at[peer] if scatter else source,
                dst_ref=landing.at[me],
                send_sem=send.at[d - 1],
                recv_sem=recv.at[d - 1],
                device_id={axis: peer},
                device_id_type=MESH,
            )
        )
    return copies


def split(value):
    high = value.astype(BF16).astype(F32)
    return high, value - high


def split3(value):
    high, rest = split(value)
    mid, low = split(rest)
    return jnp.concatenate([high, mid, low], axis=0).astype(BF16)


def thirds(value):
    n = value.shape[0] // 3
    return value[:n] + value[n : 2 * n] + value[2 * n :]


def share(n, source, landing, send, recv):
    me = lax.axis_index("seq")
    if n != 4:
        copies = sends("seq", n, source, landing, send, recv)
        for copy in copies:
            copy.start()
        landing[me] = source[...]
        for copy in copies:
            copy.wait()
        return
    pair = me + 1 - 2 * lax.rem(me, 2)
    across = lax.rem(me + 2, 4)

    def to(block, slot, peer, i):
        return pltpu.make_async_remote_copy(
            src_ref=block, dst_ref=landing.at[slot], send_sem=send.at[i], recv_sem=recv.at[i],
            device_id={"seq": peer}, device_id_type=MESH,
        )

    far, near = to(source, me, across, 0), to(source, me, pair, 1)
    far.start()
    near.start()
    landing[me] = source[...]
    far.wait_recv()
    onward = to(landing.at[across], across, pair, 2)
    onward.start()
    near.wait()
    far.wait_send()
    onward.wait()


def load_kernel(n_seq, n_tm, n_groups, head_dim, count, *refs):
    held, sems = refs[-count - 1 : -1], refs[-1]
    loads = [pltpu.make_async_copy(refs[i], held[i], sems.at[i]) for i in range(count)]
    for load in loads:
        load.start()
    picard_kernel(loads, n_seq, n_tm, n_groups, head_dim, *held, *refs[count : -count - 1])


def picard_kernel(
    loads, n_seq, n_tm, n_groups, head_dim,
    z0_ref, coef_ref, patch_ref, final_ref, terms_ref, bias_ref, qkv_ref, wo_ref,
    traj_ref, noise_ref,
    patch_t, ebuf, modbuf, wbuf, tbuf, msrc, mbuf, psrc, pbuf, asrc, abuf, bsrc, bbuf, bigt, cols,
    state, ubuf, dbuf, usrc, dsrc, yrows,
    wsend, wrecv, tsend, trecv, msend, mrecv, psend, precv, asend, arecv, bsend, brecv,
    ysend, yrecv, usend, urecv, dsend, drecv,
):
    halve = n_groups == 2 and wo_ref.shape[0] % 32 == 0
    greet([("seq", n_seq), ("tm", n_tm)] + ([("groups", n_groups)] if halve else []))
    for load in loads:
        load.wait()
    here, when = lax.axis_index("seq"), lax.axis_index("tm")
    ch, tok = z0_ref.shape
    keys = n_seq * tok
    heads_here = HEADS // n_seq
    block = heads_here * 16 + 16
    width = patch_ref.shape[1]
    rows = qkv_ref.shape[1]
    mods = bias_ref.shape[0]
    wide = bsrc.shape[1] // n_tm

    terms = sends("seq", n_seq, terms_ref, tbuf, tsend, trecv)
    for copy in terms:
        copy.start()
    if halve:
        half = wo_ref.shape[0] // 2
        group = lax.axis_index("groups")
        mine = pl.ds(pl.multiple_of(group * half, 16), half)
        outs = [
            pltpu.make_async_remote_copy(
                src_ref=wo_ref.at[mine], dst_ref=wbuf.at[when, mine],
                send_sem=wsend.at[d - 1], recv_sem=wrecv.at[d - 1],
                device_id={"tm": lax.rem(when + d, n_tm)}, device_id_type=MESH,
            )
            for d in range(1, n_tm)
        ]
    else:
        outs = sends("tm", n_tm, wo_ref, wbuf, wsend, wrecv)
    for copy in outs:
        copy.start()
    tbuf[here] = terms_ref[...]
    wbuf[when] = wo_ref[...]
    state[...] = z0_ref[...]
    bsrc[...] = jnp.zeros_like(bsrc)
    patch = patch_ref[...]
    patch_t[...] = jnp.transpose(
        jnp.concatenate([patch, jnp.zeros((128 - ch, width), F32)], axis=0)
    )[:, :ch]

    def seq_copies(it):
        return sends("seq", n_seq, usrc.at[it], ubuf.at[it], usend.at[it], urecv.at[it])

    def begin(it):
        z = state[...]
        emb = lax.dot_general(
            patch_t[...], z, (((1,), (0,)), ((), ())),
            precision=HIGH, preferred_element_type=F32,
        )
        center = emb - jnp.mean(emb, axis=0, keepdims=True)
        spread = jnp.mean(center * center, axis=0, keepdims=True)
        u = z / jnp.sqrt(spread + 1e-06)
        usrc[it] = u
        for copy in seq_copies(it):
            copy.start()
        ubuf[it, here] = u
        ebuf[...] = emb

    begin(0)
    modbuf[...] = jnp.zeros_like(modbuf)
    patch_mid = patch - jnp.mean(patch, axis=1, keepdims=True)
    mid = patch_mid[:, :rows]
    for k in range(1, n_tm):
        mid = jnp.where(when == k, patch_mid[:, k * rows : (k + 1) * rows], mid)

    def ones_tail(lanes):
        row = lax.broadcasted_iota(jnp.int32, (AUG - ch, lanes), 0)
        return jnp.where(row == 0, 1.0, 0.0).astype(F32)

    row = lax.broadcasted_iota(jnp.int32, (16, 2 * tok), 0)
    lane = lax.broadcasted_iota(jnp.int32, (16, 2 * tok), 1)
    const = jnp.where((row == 0) & (lane < tok), 1.0, 0.0).astype(BF16)
    for s in range(n_seq):
        yrows[s * block + heads_here * 16 : (s + 1) * block, :] = const

    for copy in terms:
        copy.wait()
    mod = tbuf[0]
    for s in range(1, n_seq):
        mod = mod + tbuf[s]
    mod = mod.astype(BF16).astype(F32) + bias_ref[...]
    for k in range(n_tm):
        msrc[k] = mod[:, k * rows : (k + 1) * rows]
    steps = sends("tm", n_tm, msrc, mbuf, msend, mrecv, True)
    for copy in steps:
        copy.start()
    mbuf[when] = msrc[when]
    modbuf[0:mods, :] = mod
    cols[...] = jnp.transpose(modbuf[...])
    for copy in steps:
        copy.wait()

    first = lax.broadcasted_iota(jnp.int32, (AUG - ch, rows), 0) == 0
    left = []
    for t in range(n_tm):
        step = mbuf[t]
        left.append(mid * (1.0 + step[1:2]))
        left.append(jnp.where(first, step[0:1], 0.0))
    left = split3(jnp.concatenate(left, axis=0))
    three = [thirds(jnp.dot(left, qkv_ref[j], preferred_element_type=F32)) for j in range(3)]
    rest = jnp.zeros((psrc.shape[1] - 3 * AUG, psrc.shape[2]), F32)
    for t in range(n_tm):
        piece = [part[t * AUG : (t + 1) * AUG] for part in three]
        psrc[t] = jnp.concatenate(piece + [rest], axis=0).astype(BF16)
    parts = sends("tm", n_tm, psrc, pbuf, psend, precv, True)
    for copy in parts:
        copy.start()
    pbuf[when] = psrc[when]
    swaps = []
    if halve:
        for d in range(1, n_tm):
            outs[d - 1].wait_recv()
            came = wbuf.at[lax.rem(when + n_tm - d, n_tm), mine]
            swaps.append(
                pltpu.make_async_remote_copy(
                    src_ref=came, dst_ref=came,
                    send_sem=ysend.at[d - 1], recv_sem=yrecv.at[d - 1],
                    device_id={"groups": 1 - group}, device_id_type=MESH,
                )
            )
            swaps[-1].start()
    for copy in parts:
        copy.wait()
    m_all = pbuf[0].astype(F32)
    for t in range(1, n_tm):
        m_all = m_all + pbuf[t].astype(F32)
    m_query, m_key, m_value = m_all[:AUG], m_all[AUG : 2 * AUG], m_all[2 * AUG : 3 * AUG]
    spot = lax.broadcasted_iota(jnp.int32, m_key.shape, 1)

    def own(value, h):
        at = spot[: value.shape[0]]
        return jnp.where((at >= h * head_dim) & (at < (h + 1) * head_dim), value, 0.0)

    scale = math.log2(math.e) / math.sqrt(head_dim)
    stacked = jnp.concatenate([own(m_key, h) for h in range(heads_here)], axis=0)
    asrc[...] = scale * lax.dot_general(
        stacked, m_query, (((1,), (1,)), ((), ())), precision=HIGH, preferred_element_type=F32
    )
    forms = sends("seq", n_seq, asrc, abuf, asend, arecv)
    for copy in forms:
        copy.start()
    abuf[here] = asrc[...]
    diag = [own(m_value[:ch], h) for h in range(heads_here)]
    diag += [m_value[ch:], jnp.zeros((16 - AUG + ch, m_value.shape[1]), F32)]
    diag = split3(jnp.concatenate(diag, axis=0))
    for copy in outs:
        if halve:
            copy.wait_send()
        else:
            copy.wait()
    for copy in swaps:
        copy.wait()
    for k in range(n_tm):
        bsrc[:, k * wide : k * wide + rows] = thirds(
            jnp.dot(diag, wbuf[k], preferred_element_type=F32)
        ).astype(BF16)
    share(n_seq, bsrc, bbuf, bsend, brecv)
    for copy in forms:
        copy.wait()
    compact = rows % 16 == 0
    for k in range(n_tm):
        piece = bbuf[:, :, k * wide : (k + 1) * wide].reshape(n_seq * block, wide)
        turned = jnp.transpose(piece.astype(F32)).astype(BF16)
        if compact:
            bigt[k * rows : (k + 1) * rows, :] = turned[:rows]
        else:
            bigt[k * wide : (k + 1) * wide, :] = turned
    a_all = abuf[...].reshape(HEADS * AUG, AUG)

    def one(it, carry):
        z = state[...]
        emb = ebuf[...]
        u = usrc[it]
        copies = seq_copies(it)
        u_query = jnp.concatenate([u, ones_tail(tok)], axis=0)
        g = lax.dot_general(
            a_all, u_query, (((1,), (0,)), ((), ())),
            precision=HIGH, preferred_element_type=F32,
        )
        for copy in copies:
            copy.wait()
        u_all = jnp.concatenate([ubuf[it, s] for s in range(n_seq)], axis=1)
        u_keys = jnp.concatenate([u_all, ones_tail(keys)], axis=0)
        k_high, k_low = split(u_keys)
        pad = jnp.zeros((128 - 3 * AUG, keys), F32)
        key_rows = jnp.transpose(jnp.concatenate([k_high, k_high, k_low, pad], axis=0)).astype(BF16)
        values = jnp.concatenate([k_high, k_low], axis=0).astype(BF16)
        qpad = jnp.zeros((128 - 3 * AUG, 2 * tok), F32)
        for pair in range(HEADS // 2):
            lo = pair * 2 * AUG
            both = jnp.concatenate([g[lo : lo + AUG], g[lo + AUG : lo + 2 * AUG]], axis=1)
            q_high, q_low = split(both)
            query = jnp.concatenate([q_high, q_low, q_high, qpad], axis=0).astype(BF16)
            scores = jnp.dot(key_rows, query, preferred_element_type=F32)
            top = jnp.max(scores, axis=0, keepdims=True)
            probs = jnp.exp2(scores - top).astype(BF16)
            out = jnp.dot(values, probs, preferred_element_type=F32)
            out = out[:AUG] + out[AUG:]
            y_high, y_low = split(out[:ch] / out[ch : ch + 1])
            for k in range(2):
                head = pair * 2 + k
                at = head // heads_here * block + head % heads_here * 16
                cut = slice(k * tok, (k + 1) * tok)
                yrows[at : at + 16, 0:tok] = y_high[:, cut].astype(BF16)
                yrows[at : at + 16, tok : 2 * tok] = y_low[:, cut].astype(BF16)
        proj = jnp.dot(bigt[...], yrows[...], preferred_element_type=F32)
        proj = proj[:, :tok] + proj[:, tok:]
        if not compact:
            proj = jnp.concatenate(
                [proj[k * wide : k * wide + rows] for k in range(n_tm)], axis=0
            )
        residual = emb + cols[:, 2:3] * proj
        center = residual - jnp.mean(residual, axis=0, keepdims=True)
        spread = jnp.mean(center * center, axis=0, keepdims=True)
        normed = center / jnp.sqrt(spread + 1e-06)
        final_in = (normed * (1.0 + cols[:, 4:5]) + cols[:, 3:4]).astype(BF16)
        noise = jnp.dot(final_ref[...], final_in, preferred_element_type=F32)
        noise_ref[...] = noise
        drift = coef_ref[0] * z + coef_ref[1] * noise
        dsrc[it] = drift
        copies = sends("tm", n_tm, dsrc.at[it], dbuf.at[it], dsend.at[it], drecv.at[it])
        for copy in copies:
            copy.start()
        dbuf[it, when] = drift
        for copy in copies:
            copy.wait()
        total = jnp.zeros_like(drift)
        for j in range(n_tm - 1):
            total = total + jnp.where(when > j, dbuf[it, j], 0.0)
        state[...] = z0_ref[...] + total

        @pl.when(it < ITERS - 1)
        def _():
            begin(it + 1)

        return carry

    lax.fori_loop(0, ITERS, one, 0)
    traj_ref[...] = state[...]


def picard(head_dim, z0, coef, patch, final_t, terms, bias, qkv, wo):
    n_seq, n_tm = lax.axis_size("seq"), lax.axis_size("tm")
    ch, tok = z0.shape
    width = patch.shape[1]
    rows, here = qkv.shape[1], wo.shape[0]
    mods = bias.shape[0]
    values = (z0, coef, patch, final_t, terms, bias, qkv, wo)
    part_rows = -(-3 * AUG // 16) * 16
    block = HEADS // n_seq * 16 + 16
    wide = -(-rows // 128) * 128
    vmem = pl.BlockSpec(memory_space=pltpu.VMEM)
    sem, mem = pltpu.SemaphoreType.DMA, pltpu.VMEM
    pairs = []
    for n in (n_tm, n_seq, n_tm, n_tm, n_seq, n_seq, n_tm):
        pairs += [sem((n - 1,)), sem((n - 1,))]
    for n in (n_seq, n_tm):
        pairs += [sem((ITERS, n - 1)), sem((ITERS, n - 1))]
    return pl.pallas_call(
        functools.partial(
            load_kernel, n_seq, n_tm, lax.axis_size("groups"), head_dim, len(values)
        ),
        out_shape=[jax.ShapeDtypeStruct((ch, tok), F32)] * 2,
        in_specs=[pl.BlockSpec(memory_space=pl.ANY)] * len(values),
        out_specs=[vmem] * 2,
        scratch_shapes=[
            mem((width, ch), F32),
            mem((width, tok), F32),
            mem((128, width), F32),
            mem((n_tm,) + wo.shape, BF16),
            mem((n_seq,) + terms.shape, F32),
            mem((n_tm, mods, rows), F32),
            mem((n_tm, mods, rows), F32),
            mem((n_tm, part_rows, here), BF16),
            mem((n_tm, part_rows, here), BF16),
            mem((HEADS // n_seq * AUG, AUG), F32),
            mem((n_seq, HEADS // n_seq * AUG, AUG), F32),
            mem((block, n_tm * wide), BF16),
            mem((n_seq, block, n_tm * wide), BF16),
            mem((width if rows % 16 == 0 else n_tm * wide, n_seq * block), BF16),
            mem((width, 128), F32),
            mem((ch, tok), F32),
            mem((ITERS, n_seq, ch, tok), F32),
            mem((ITERS, n_tm, ch, tok), F32),
            mem((ITERS, ch, tok), F32),
            mem((ITERS, ch, tok), F32),
            mem((n_seq * block, 2 * tok), BF16),
        ] + pairs + [mem(v.shape, v.dtype) for v in values] + [sem((len(values),))],
        compiler_params=pltpu.CompilerParams(
            collective_id=0, has_side_effects=True, vmem_limit_bytes=56 << 20
        ),
    )(*values)


def plan_coefs(beta_table, cur_ids, next_ids):
    keep = 1.0 - beta_table
    pos = jnp.arange(beta_table.shape[0], dtype=jnp.int32)
    bar_now = jnp.prod(jnp.where(pos[None] <= cur_ids[:, None], keep[None], 1.0), axis=1)
    bar_next = jnp.prod(jnp.where(pos[None] <= next_ids[:, None], keep[None], 1.0), axis=1)
    coef_a = jnp.sqrt(bar_next / bar_now)
    coef_b = jnp.sqrt(1.0 - bar_next) - coef_a * jnp.sqrt(1.0 - bar_now)
    return (coef_a, coef_b)


def frequency_embed(cur_ids, freq_width):
    half = freq_width // 2
    freqs = jnp.exp(-math.log(10000.0) * jnp.arange(half, dtype=F32) / half)
    angles = cur_ids.astype(F32)[:, None] * freqs[None, :]
    return jnp.concatenate([jnp.cos(angles), jnp.sin(angles)], axis=1)


def body(
    init_latent, cur_ids, next_ids, beta_table, temb_weight, mod_weight, mod_bias,
    patch_weight, qkv_weight, out_weight, final_weight,
):
    ch, width = patch_weight.shape
    tok = init_latent.shape[1]
    here = lax.axis_index("seq")
    cols = qkv_weight.shape[2]

    coef_a, coef_b = plan_coefs(beta_table, cur_ids, next_ids)
    coef = jnp.broadcast_to(
        jnp.stack([coef_a[0] - 1.0, coef_b[0]])[:, None, None], (2, ch, tok)
    )
    freq_emb = frequency_embed(cur_ids, temb_weight.shape[0]).astype(BF16)
    feats = mod_weight.shape[0]
    temb_here = lax.dynamic_slice_in_dim(temb_weight, here * feats, feats, 1)
    emb_part = jax.nn.silu(jnp.dot(freq_emb, temb_here, preferred_element_type=F32)).astype(BF16)
    mod_terms = jnp.einsum("d,dme->me", emb_part[0], mod_weight, preferred_element_type=F32)
    traj, noise = picard(
        width // HEADS, init_latent, coef, patch_weight, final_weight.T, mod_terms, mod_bias,
        jnp.swapaxes(qkv_weight, 0, 1),
        lax.dynamic_slice_in_dim(out_weight, here * cols, cols, 0),
    )
    return (traj[None], noise[None])


def solution(mesh):
    in_specs = (
        P("groups", "seq"),
        P("tm"),
        P("tm"),
        P(),
        P(),
        P("seq", None, None),
        P(),
        P(),
        P("tm", None, "seq"),
        P(None, "tm"),
        P(),
    )
    out_specs = (P("tm", "groups", "seq"), P("tm", "groups", "seq"))
    return jax.shard_map(body, mesh=mesh, in_specs=in_specs, out_specs=out_specs, check_vma=False)
```
